32 devices in a mesh: rows: 8 (over z, x), grp: 4 (over y, core).
Axes of the slice: x: 2, y: 2, z: 4, core: 2. Of those that a mesh axis runs over, the one named last changes fastest.
Arguments:
- a_blocks: float32 [256, 7, 128, 128], P(('rows', 'grp')), may hold values from -0.5 to 0.5
- neighbours: int32 [256, 7], P(('rows', 'grp')), may hold values from 0 to 255, as said below
- neighbour_count: int32 [256], P(('rows', 'grp')), may hold values from 1 to 7
- p_blocks: float32 [256, 2, 128, 128], P(('rows', 'grp')), may hold values from -1 to 1
- p_columns: int32 [256, 2], P(('rows', 'grp')), may hold values from 0 to 31, as said below
- p_count: int32 [256], P(('rows', 'grp')), may hold values from 1 to 2
- coarse_slot: int32 [32], replicated, may hold values from 0 to 3, as said below
- coarse_pattern: int32 [32, 4], replicated, may hold values from 0 to 31, as said below
Outputs:
- coarse_op: float32 [32, 4, 128, 128], P(('rows', 'grp'))
The draws below stay inside these ranges and needn't reach their ends.
Inputs may be any that keep to these rules, and one draw needn't show every extreme that they name: neighbours[e,0] = e; every neighbour of an element of the slab of 32 elements that holds it lies in that slab or within 8 elements before or after it. The elements of slab q form aggregates q * 4 to (q + 1) * 4 - 1, eight elements each; p_columns[e,0] is the aggregate of e, and every slot names an aggregate of the element's slab or of a slab beside it. `coarse_slot`: within each slab the aggregates take each position 0 to 3 once. coarse_pattern[c,0] = c; every column is an aggregate of c's slab or of a slab beside it; columns may repeat.
All inputs are finite; a program needn't handle non-finite values.
Results may differ from the reference program's by a relative error of at most 0.0003.
Values sent between devices are 32-bit elements; how exact they have to be, the bound alone decides.
No kernel may reach another device: no remote copies, remote signals or barrier semaphores. Data moves between devices by JAX's collectives and lax.ppermute only.
A program may use at most 64 MiB of HBM per device.

```python
import jax
import jax.numpy as jnp
from jax import lax

B = 128
K = 7
KP = 2
KC = 4
SLAB = 32
AGG_SLAB = 4
RIM = 8
NE = 256
NAGG = 32


def slab_permutation(key, count, length):
    scores = jax.random.randint(key, (count, length), 0, 1 << 20) * length + jnp.arange(length, dtype=jnp.int32)[None, :]
    return jnp.argsort(scores, axis=1).astype(jnp.int32)


def draw_neighbours(key, part):
    element = jnp.arange(NE, dtype=jnp.int32)
    slab_id = element // SLAB
    lower = jnp.maximum(slab_id * SLAB - RIM, 0)
    upper = jnp.minimum((slab_id + 1) * SLAB + RIM, NE)
    picks = jax.random.randint(key, (NE, K), lower[:, None], upper[:, None])
    return picks.at[:, 0].set(element).astype(jnp.int32)


def draw_neighbour_count(key, part):
    base = jax.random.randint(key, (NE,), 1, K + 1)
    index = jnp.arange(NE, dtype=jnp.int32)
    return jnp.where(index % 7 == 0, K, jnp.where(index % 7 == 1, 1, base)).astype(jnp.int32)


def draw_p_count(key, part):
    base = jax.random.randint(key, (NE,), 1, KP + 1)
    index = jnp.arange(NE, dtype=jnp.int32)
    return jnp.where(index % 5 == 0, KP, jnp.where(index % 5 == 1, 1, base)).astype(jnp.int32)


def draw_p_columns(key, part):
    slab_total = NE // SLAB
    order = slab_permutation(jax.random.fold_in(key, 11), slab_total, SLAB)
    slab_id = jnp.arange(NE, dtype=jnp.int32) // SLAB
    own = slab_id * AGG_SLAB + (order // 8).reshape(NE)
    lower = jnp.maximum(slab_id - 1, 0) * AGG_SLAB
    upper = jnp.minimum(slab_id + 2, slab_total) * AGG_SLAB
    others = jax.random.randint(jax.random.fold_in(key, 12), (NE, KP - 1), lower[:, None], upper[:, None])
    return jnp.concatenate([own[:, None], others], axis=1).astype(jnp.int32)


def draw_coarse_slot(key, part):
    order = slab_permutation(key, NAGG // AGG_SLAB, AGG_SLAB)
    return order.reshape(NAGG).astype(jnp.int32)


def draw_coarse_pattern(key, part):
    slab_total = NAGG // AGG_SLAB
    agg = jnp.arange(NAGG, dtype=jnp.int32)
    slab_id = agg // AGG_SLAB
    lower = jnp.maximum(slab_id - 1, 0) * AGG_SLAB
    upper = jnp.minimum(slab_id + 2, slab_total) * AGG_SLAB
    others = jax.random.randint(key, (NAGG, KC - 1), lower[:, None], upper[:, None])
    return jnp.concatenate([agg[:, None], others], axis=1).astype(jnp.int32)


def levels(stream_key, shape, split, low, high):
    loudness, own = 1.0, jax.random.fold_in(stream_key, 6)
    for axis_at, shards_of in split:
        draws = jnp.exp(jax.random.uniform(jax.random.fold_in(own, axis_at), (shards_of,), jnp.float32, low / len(split), high / len(split)))
        loudness = loudness * jnp.repeat(draws, shape[axis_at] // shards_of).reshape([-1 if axis == axis_at else 1 for axis in range(len(shape))])
    return loudness


def noise(stream_key, extent, spread, reach, shards=(), held_as=jnp.bfloat16):
    result = spread * jax.random.normal(stream_key, extent, jnp.float32)
    if shards:
        result = result * levels(stream_key, extent, shards, -0.22, 0.18)
    return jnp.clip(result, -reach, reach).astype(held_as)


def setup_inputs(seed: int = 0) -> dict:
    seeds = jax.random.split(jax.random.key(seed), 9)
    a_blocks = noise(seeds[0], (NE, K, B, B), B ** -0.5, 0.5, ((0, 32),), jnp.float32)
    neighbours = draw_neighbours(jax.random.fold_in(seeds[8], 71), 0)
    neighbour_count = draw_neighbour_count(jax.random.fold_in(seeds[8], 71), 0)
    p_blocks = noise(seeds[3], (NE, KP, B, B), 0.17, 1.0, ((0, 32),), jnp.float32)
    p_columns = draw_p_columns(jax.random.fold_in(seeds[8], 71), 0)
    p_count = draw_p_count(jax.random.fold_in(seeds[8], 71), 0)
    coarse_slot = draw_coarse_slot(jax.random.fold_in(seeds[8], 71), 0)
    coarse_pattern = draw_coarse_pattern(jax.random.fold_in(seeds[8], 71), 0)
    return dict(a_blocks=a_blocks, neighbours=neighbours, neighbour_count=neighbour_count, p_blocks=p_blocks, p_columns=p_columns, p_count=p_count, coarse_slot=coarse_slot, coarse_pattern=coarse_pattern)


HIGH = lax.Precision.HIGHEST


def reference(a_blocks, neighbours, neighbour_count, p_blocks, p_columns, p_count, coarse_slot, coarse_pattern):
    slab_count = NE // SLAB

    def one_slab(galerkin, slab_id):
        start = (slab_id * SLAB).astype(jnp.int32)
        blocks = lax.dynamic_slice_in_dim(a_blocks, start, SLAB, 0)
        near = lax.dynamic_slice_in_dim(neighbours, start, SLAB, 0)
        near_count = lax.dynamic_slice_in_dim(neighbour_count, start, SLAB, 0)
        own_p = lax.dynamic_slice_in_dim(p_blocks, start, SLAB, 0)
        own_cols = lax.dynamic_slice_in_dim(p_columns, start, SLAB, 0)
        own_count = lax.dynamic_slice_in_dim(p_count, start, SLAB, 0)
        near_p = jnp.take(p_blocks, near, axis=0)
        near_cols = jnp.take(p_columns, near, axis=0)
        near_live = jnp.arange(KP, dtype=jnp.int32)[None, None, :] < jnp.take(p_count, near, axis=0)[:, :, None]
        slot_live = jnp.arange(K, dtype=jnp.int32)[None, :] < near_count[:, None]
        own_live = jnp.arange(KP, dtype=jnp.int32)[None, :] < own_count[:, None]
        products = jnp.einsum('ekab,ekjbc->ekjac', blocks, near_p, precision=HIGH)
        targets = jnp.take(coarse_pattern, own_cols, axis=0)
        select = (slot_live[:, None, None, :, None] & own_live[:, :, None, None, None]
                  & near_live[:, None, None, :, :]
                  & (near_cols[:, None, None, :, :] == targets[:, :, :, None, None])).astype(jnp.float32)
        summed = jnp.einsum('ejskl,eklac->ejsac', select, products, precision=HIGH)
        terms = jnp.einsum('ejba,ejsbc->ejsac', own_p, summed, precision=HIGH)
        galerkin = galerkin.at[own_cols.reshape(-1)].add(terms.reshape(SLAB * KP, KC, B, B))
        return galerkin, None

    start_value = jnp.zeros((NAGG, KC, B, B), jnp.float32)
    galerkin, unused = lax.scan(one_slab, start_value, jnp.arange(slab_count, dtype=jnp.int32))
    places = (jnp.arange(NAGG, dtype=jnp.int32) // AGG_SLAB) * AGG_SLAB + coarse_slot
    return jnp.zeros((NAGG, KC, B, B), jnp.float32).at[places].set(galerkin)
```

```python
import functools

import jax
import jax.numpy as jnp
from jax import lax
from jax.experimental import pallas as pl
from jax.experimental.pallas import tpu as pltpu
from jax.sharding import PartitionSpec as P

UNROLL = 4


def split(value):
    high = value.astype(jnp.bfloat16)
    low = (value - high.astype(jnp.float32)).astype(jnp.bfloat16)
    return high, low


def left_kernel(a_ref, p_ref, q_ref):
    slots, size = p_ref.shape[1], p_ref.shape[2]
    rows = []
    for j in range(slots):
        high, low = split(p_ref[0, j].T)
        rows.append(jnp.concatenate([high, high, low], axis=1))
    left = jnp.concatenate(rows, axis=0)
    for k in range(a_ref.shape[1]):
        high, low = split(a_ref[0, k])
        right = jnp.concatenate([high, low, high], axis=0)
        product = jnp.dot(left, right, preferred_element_type=jnp.float32)
        for j in range(slots):
            q_ref[0, j, k] = product[j * size : (j + 1) * size]


def left_products(a_blocks, p_blocks):
    count, near, size, _ = a_blocks.shape
    slots = p_blocks.shape[1]
    return pl.pallas_call(
        left_kernel,
        grid=(count,),
        in_specs=[
            pl.BlockSpec((1, near, size, size), lambda e: (e, 0, 0, 0)),
            pl.BlockSpec((1, slots, size, size), lambda e: (e, 0, 0, 0)),
        ],
        out_specs=pl.BlockSpec((1, slots, near, size, size), lambda e: (e, 0, 0, 0, 0)),
        out_shape=jax.ShapeDtypeStruct((count, slots, near, size, size), jnp.float32),
        compiler_params=pltpu.CompilerParams(vmem_limit_bytes=32 * 1024 * 1024),
        cost_estimate=pl.CostEstimate(
            flops=2 * 3 * count * near * slots * size**3,
            bytes_accessed=4 * size * size * count * (near + slots + near * slots),
            transcendentals=0,
        ),
        name="left_products",
    )(a_blocks, p_blocks)


def bits(count):
    return max(1, (count - 1).bit_length())


def list_kernel(
    sizes, place, near_ref, near_count, cols, col_count, slot_of, pattern, mine, theirs, list_ref, total_ref
):
    e_local, n_slot, p_slot, pat, groups, agg_slab = sizes
    blocks = e_local * p_slot
    p_bits, o_bits = bits(8 * blocks), bits(12 * (agg_slab // groups) * pat + 1)
    row, grp = place[0], place[1]
    core = lax.bitwise_and(grp, 1)
    edge = jnp.logical_or(grp == 0, grp == groups - 1)
    per_owner = agg_slab // groups

    def over_e(e, found):
        def over_k(k, found):
            n = near_ref[e, k]
            home = n // e_local
            inner = n - home * e_local
            home_row = home // groups
            offset = home_row - row
            crossed = lax.bitwise_xor(home - home_row * groups, grp)
            in_slab = offset == 0
            rim_theirs = jnp.where(offset < 0, 1 - core, core)
            part = jnp.where(in_slab, lax.shift_right_logical(crossed, 1), 2)
            other = jnp.where(in_slab, lax.bitwise_and(crossed, 1), rim_theirs)
            rim_buffer = jnp.where(
                rim_theirs == 0, jnp.where(edge, 4, 5), jnp.where(edge, 7, 6)
            )
            buffer = jnp.where(in_slab, crossed, rim_buffer)

            def over_l(l, found):
                at = inner * p_slot + l
                d = jnp.where(other == 0, mine[part, at], theirs[part, at])

                def over_j(j, found):
                    c = cols[e, j]
                    slab_at = c // agg_slab - row + 1
                    owner = lax.bitwise_xor(slot_of[c] // per_owner, grp)
                    inner_slot = lax.rem(slot_of[c], per_owner)
                    half = lax.bitwise_and(owner, 1)
                    upper = lax.shift_right_logical(owner, 1)
                    out = ((half * 2 + upper) * 3 + slab_at) * per_owner + inner_slot
                    q = (e * p_slot + j) * n_slot + k
                    code = ((q << p_bits) + (buffer * blocks + at) << o_bits) + out * pat
                    for s in range(pat):
                        list_ref[found] = code + s
                        found = found + (pattern[c, s] == d).astype(jnp.int32)
                    return found

                return lax.fori_loop(0, jnp.where(d >= 0, col_count[e], 0), over_j, found)

            return lax.fori_loop(0, p_slot, over_l, found)

        return lax.fori_loop(0, near_count[e], over_k, found)

    found = lax.fori_loop(0, e_local, over_e, jnp.int32(0))
    total_ref[0] = found
    for pad in range(UNROLL):
        list_ref[found + pad] = 12 * per_owner * pat


def tuple_list(place, neighbours, neighbour_count, p_columns, p_count, coarse_slot, pattern, mine, theirs, groups, agg_slab):
    e_local, n_slot = neighbours.shape
    p_slot, pat = p_columns.shape[1], pattern.shape[1]
    sizes = (e_local, n_slot, p_slot, pat, groups, agg_slab)
    longest = e_local * n_slot * p_slot * p_slot * pat + UNROLL
    smem = pl.BlockSpec(memory_space=pltpu.SMEM)
    return pl.pallas_call(
        functools.partial(list_kernel, sizes),
        in_specs=[smem] * 9,
        out_specs=[smem] * 2,
        out_shape=[jax.ShapeDtypeStruct((longest,), jnp.int32), jax.ShapeDtypeStruct((1,), jnp.int32)],
        cost_estimate=pl.CostEstimate(flops=4000000, bytes_accessed=4000000, transcendentals=0),
        name="tuple_list",
    )(place, neighbours, neighbour_count, p_columns, p_count, coarse_slot, pattern, mine, theirs)


def sum_kernel(sizes, list_ref, total_ref, q_ref, *refs):
    blocks, kept = sizes
    p_refs, (keep, send, acc, q_buf, p_buf, sems, out_sems) = refs[:8], refs[8:]
    p_bits, o_bits = bits(8 * blocks), bits(2 * kept + 1)
    size = q_ref.shape[-1]

    def fetch(chunk, slot):
        for u in range(UNROLL):
            code = lax.shift_right_logical(list_ref[chunk * UNROLL + u], o_bits)
            q = lax.shift_right_logical(code, p_bits)
            at = lax.bitwise_and(code, (1 << p_bits) - 1)
            buffer = at // blocks
            inner = at - buffer * blocks
            pltpu.make_async_copy(q_ref.at[q], q_buf.at[slot, u], sems.at[slot, u, 0]).start()
            for b in range(8):

                @pl.when(buffer == b)
                def _():
                    pltpu.make_async_copy(
                        p_refs[b].at[inner], p_buf.at[slot, u], sems.at[slot, u, 1]
                    ).start()

    chunks = (total_ref[0] + UNROLL - 1) // UNROLL

    @pl.when(chunks > 0)
    def _():
        fetch(0, 0)

    def clear(i, carry):
        acc[i] = jnp.zeros((size, size), jnp.float32)
        return carry

    lax.fori_loop(0, 2 * kept + 1, clear, 0)

    def step(chunk, carry):
        slot = lax.rem(chunk, 2)

        @pl.when(chunk + 1 < chunks)
        def _():
            fetch(chunk + 1, 1 - slot)

        products = []
        for u in range(UNROLL):
            pltpu.make_async_copy(q_ref.at[0], q_buf.at[slot, u], sems.at[slot, u, 0]).wait()
            pltpu.make_async_copy(p_refs[0].at[0], p_buf.at[slot, u], sems.at[slot, u, 1]).wait()
        for u in range(UNROLL):
            q_high, q_low = split(q_buf[slot, u])
            p_high, p_low = split(p_buf[slot, u])
            left = jnp.concatenate([q_high, q_high, q_low], axis=1)
            right = jnp.concatenate([p_high, p_low, p_high], axis=0)
            products.append(jnp.dot(left, right, preferred_element_type=jnp.float32))
        for u in range(UNROLL):
            out = lax.bitwise_and(list_ref[chunk * UNROLL + u], (1 << o_bits) - 1)
            acc[out] += products[u]
        return carry

    lax.fori_loop(0, chunks, step, 0)
    first = pltpu.make_async_copy(acc.at[pl.ds(kept, kept)], send, out_sems.at[0])
    second = pltpu.make_async_copy(acc.at[pl.ds(0, kept)], keep, out_sems.at[1])
    first.start()
    second.start()
    first.wait()
    second.wait()


def tuple_sums(entries, total, q_blocks, p_buffers, kept):
    size = q_blocks.shape[-1]
    blocks = p_buffers[0].shape[0]
    smem = pl.BlockSpec(memory_space=pltpu.SMEM)
    anywhere = pl.BlockSpec(memory_space=pl.ANY)
    return pl.pallas_call(
        functools.partial(sum_kernel, (blocks, kept)),
        in_specs=[smem, smem] + [anywhere] * 9,
        out_specs=[anywhere] * 2,
        out_shape=[jax.ShapeDtypeStruct((kept, size, size), jnp.float32)] * 2,
        scratch_shapes=[
            pltpu.VMEM((2 * kept + 1, size, size), jnp.float32),
            pltpu.VMEM((2, UNROLL, size, size), jnp.float32),
            pltpu.VMEM((2, UNROLL, size, size), jnp.float32),
            pltpu.SemaphoreType.DMA((2, UNROLL, 2)),
            pltpu.SemaphoreType.DMA((2,)),
        ],
        compiler_params=pltpu.CompilerParams(vmem_limit_bytes=32 * 1024 * 1024),
        cost_estimate=pl.CostEstimate(flops=10**9, bytes_accessed=10**7, transcendentals=0),
        name="tuple_sums",
    )(entries, total, q_blocks, *p_buffers)


def per_device(
    a_blocks, neighbours, neighbour_count, p_blocks, p_columns, p_count, coarse_slot, coarse_pattern
):
    rows, groups = lax.axis_size("rows"), lax.axis_size("grp")
    e_local, n_slot, size = a_blocks.shape[:3]
    p_slot = p_blocks.shape[1]
    pat = coarse_pattern.shape[1]
    agg_slab = coarse_slot.shape[0] // rows
    row, grp = lax.axis_index("rows"), lax.axis_index("grp")
    upper = groups // 2
    core_pairs = [(g, g ^ 1) for g in range(groups)]
    upper_pairs = [(g, g ^ upper) for g in range(groups)]

    def along(g, step):
        return [
            (r * groups + g, (r + step) * groups + g)
            for r in range(rows)
            if 0 <= r + step < rows
        ]

    first, last = 0, groups - 1
    direct = along(last, 1) + along(first, -1)
    forwarded = along(last ^ upper, 1) + along(first ^ upper, -1)
    both = ("rows", "grp")

    live = jnp.arange(p_slot, dtype=jnp.int32)[None, :] < p_count[:, None]
    own_cols = jnp.where(live, p_columns, -1).reshape(e_local * p_slot)
    across_cols = lax.ppermute(own_cols, "grp", upper_pairs)
    is_edge = (grp == first) | (grp == last)
    rim_cols = lax.ppermute(jnp.where(is_edge, own_cols, across_cols), both, direct + forwarded)
    mine = jnp.stack([own_cols, across_cols, rim_cols])
    theirs = lax.ppermute(mine, "grp", core_pairs)

    own = p_blocks.reshape(e_local * p_slot, size, size)
    across = lax.ppermute(own, "grp", upper_pairs)
    rim = lax.ppermute(own, both, direct)
    own_core = lax.ppermute(own, "grp", core_pairs)
    rim_core = lax.ppermute(rim, "grp", [(first, first ^ 1), (last, last ^ 1)])
    rim_far = lax.ppermute(across, both, forwarded)
    across_core = lax.ppermute(across, "grp", core_pairs)
    rim_far_core = lax.ppermute(
        rim_far, "grp", [(first ^ upper, first ^ upper ^ 1), (last ^ upper, last ^ upper ^ 1)]
    )

    place = jnp.stack([row, grp]).astype(jnp.int32)
    entries, total = tuple_list(
        place, neighbours, neighbour_count, p_columns, p_count, coarse_slot, coarse_pattern, mine, theirs, groups, agg_slab
    )
    q_blocks = left_products(a_blocks, p_blocks).reshape(e_local * p_slot * n_slot, size, size)
    per_owner = agg_slab // groups
    kept = 2 * 3 * per_owner * pat
    keep, send = tuple_sums(
        entries,
        total,
        q_blocks,
        [own, own_core, across, across_core, rim, rim_far, rim_core, rim_far_core],
        kept,
    )
    shape = (2, 3, per_owner, pat, size, size)
    chip = keep.reshape(shape) + lax.ppermute(send, "grp", core_pairs).reshape(shape)
    down, here, up = (
        chip[0, t] + lax.ppermute(chip[1, t], "grp", upper_pairs) for t in range(3)
    )
    from_next = lax.ppermute(down, "rows", [(r, r - 1) for r in range(1, rows)])
    from_prev = lax.ppermute(up, "rows", [(r, r + 1) for r in range(rows - 1)])
    return here + from_next + from_prev


def solution(mesh):
    return jax.shard_map(
        per_device,
        mesh=mesh,
        in_specs=(
            P(("rows", "grp"), None, None, None),
            P(("rows", "grp"), None),
            P(("rows", "grp")),
            P(("rows", "grp"), None, None, None),
            P(("rows", "grp"), None),
            P(("rows", "grp")),
            P(),
            P(),
        ),
        out_specs=P(("rows", "grp"), None, None, None),
        check_vma=False,
    )
```

```python
import functools

import jax
import jax.numpy as jnp
from jax import lax
from jax.experimental import pallas as pl
from jax.experimental.pallas import tpu as pltpu
from jax.sharding import PartitionSpec as P

UNROLL = 4
BUFFERS = 6
VMEM_LIMIT = 8 * 1024 * 1024


def split(value):
    high = value.astype(jnp.bfloat16)
    low = (value - high.astype(jnp.float32)).astype(jnp.bfloat16)
    return high, low


def work(microseconds):
    return pl.CostEstimate(flops=microseconds * 10**9, bytes_accessed=microseconds * 10**6, transcendentals=0)


def bits(count):
    return max(1, (count - 1).bit_length())


class Layout:
    def __init__(self, e_local, n_slot, p_slot, size, pat, groups, agg_slab):
        self.e_local, self.n_slot, self.p_slot, self.size, self.pat = e_local, n_slot, p_slot, size, pat
        self.groups, self.agg_slab, self.per_owner = groups, agg_slab, agg_slab // groups
        self.blocks = e_local * p_slot
        self.near_at = 0
        self.near_count_at = e_local * n_slot
        self.cols_at = self.near_count_at + e_local
        self.col_count_at = self.cols_at + self.blocks
        self.live_at = self.col_count_at + e_local
        self.longest = 2 * e_local * n_slot * p_slot * p_slot * pat + UNROLL
        self.most_q = 2 * e_local * p_slot * n_slot + 2 * UNROLL
        self.row_blocks = self.per_owner * pat
        self.outs = 6 * self.row_blocks
        self.p_bits, self.o_bits = bits(self.blocks), bits(self.outs + 1)


def list_kernel(lay, place, mine, theirs, slot_of, pattern, list_ref, count_ref, q_list, need_ref):
    row, grp = place[0], place[1]
    core = lax.bitwise_and(grp, 1)
    edge = jnp.logical_or(grp == 0, grp == lay.groups - 1)
    for b in range(BUFFERS):
        count_ref[b] = 0

    def scan(side, first_q):
        meta = (mine, theirs)[side]

        def over_e(e, q_found):
            for j in range(lay.p_slot):
                need_ref[side * lay.blocks + e * lay.p_slot + j] = 0

            def over_j(j, q_found):
                c = meta[lay.cols_at + e * lay.p_slot + j]
                slot = slot_of[c]
                owner = lax.bitwise_xor(slot // lay.per_owner, grp)
                upper = lax.shift_right_logical(owner, 1)
                slab_at = c // lay.agg_slab - row + 1
                out = ((upper * 3 + slab_at) * lay.per_owner + lax.rem(slot, lay.per_owner)) * lay.pat
                wanted = [pattern[c * lay.pat + s] for s in range(lay.pat)]
                ej = e * lay.p_slot + j
                ours = lax.bitwise_and(owner, 1) == 0
                need_ref[side * lay.blocks + ej] = ours.astype(jnp.int32)

                def over_k(k, q_found):
                    n = meta[lay.near_at + e * lay.n_slot + k]
                    home = n // lay.e_local
                    inner = n - home * lay.e_local
                    home_row = home // lay.groups
                    offset = home_row - row
                    crossed = lax.bitwise_xor(home - home_row * lay.groups, grp)
                    in_slab = offset == 0
                    rim_other = jnp.where(offset < 0, 1 - core, core)
                    other = jnp.where(in_slab, lax.bitwise_and(crossed, 1), rim_other)
                    holder_edge = jnp.logical_xor(edge, other == 1)
                    far = jnp.logical_and(in_slab, crossed >= 2)
                    rim = jnp.logical_not(in_slab)
                    late = jnp.where(holder_edge, far, rim)
                    part = jnp.where(jnp.logical_and(in_slab, crossed < 2), 0, jnp.where(late, 2, 1))
                    field = jnp.where(in_slab, lax.shift_right_logical(crossed, 1), 2)
                    buffer = part * 2 + other
                    at = inner * lay.p_slot
                    field_at = lay.live_at + field * lay.blocks + at
                    found = count_ref[buffer]
                    start = found
                    base = buffer * lay.longest
                    for l in range(lay.p_slot):
                        d = jnp.where(other == 0, mine[field_at + l], theirs[field_at + l])
                        code = ((((q_found << lay.p_bits) + at + l) << lay.o_bits) + out)
                        for s in range(lay.pat):
                            list_ref[base + found] = code + s
                            found = found + (wanted[s] == d).astype(jnp.int32)
                    count_ref[buffer] = found
                    q_list[q_found] = ej * lay.n_slot + k
                    return q_found + (found > start).astype(jnp.int32)

                live_near = jnp.where(ours, meta[lay.near_count_at + e], 0)
                return lax.fori_loop(0, live_near, over_k, q_found)

            return lax.fori_loop(0, meta[lay.col_count_at + e], over_j, q_found)

        q_found = lax.fori_loop(0, lay.e_local, over_e, first_q)
        for u in range(UNROLL):
            q_list[q_found + u] = 0
        return (q_found + UNROLL - 1) // UNROLL

    middle = scan(0, jnp.int32(0))
    count_ref[BUFFERS] = middle
    count_ref[BUFFERS + 1] = scan(1, middle * UNROLL)
    for b in range(BUFFERS):
        for u in range(UNROLL):
            list_ref[b * lay.longest + count_ref[b] + u] = lay.outs


def match_lists(lay, place, mine, theirs, coarse_slot, pattern):
    smem = pl.BlockSpec(memory_space=pltpu.SMEM)
    return pl.pallas_call(
        functools.partial(list_kernel, lay),
        in_specs=[smem] * 5,
        out_specs=[smem] * 4,
        out_shape=[
            jax.ShapeDtypeStruct((BUFFERS * lay.longest,), jnp.int32),
            jax.ShapeDtypeStruct((BUFFERS + 2,), jnp.int32),
            jax.ShapeDtypeStruct((lay.most_q + UNROLL,), jnp.int32),
            jax.ShapeDtypeStruct((2 * lay.blocks,), jnp.int32),
        ],
        compiler_params=pltpu.CompilerParams(vmem_limit_bytes=1024 * 1024),
        cost_estimate=work(4),
        name="match_lists",
    )(place, mine, theirs, coarse_slot, pattern)


def left_kernel(lay, count_ref, q_list, need_ref, a_mine, a_theirs, p_mine, p_theirs, q_ref, left_ref):
    for side, p_ref in enumerate((p_mine, p_theirs)):

        def prepare(ej, carry, side=side, p_ref=p_ref):
            @pl.when(need_ref[side * lay.blocks + ej] == 1)
            def _():
                high, low = split(p_ref[ej].T)
                left_ref[side * lay.blocks + ej] = jnp.concatenate([high, high, low], axis=1)

            return carry

        lax.fori_loop(0, lay.blocks, prepare, 0)

    def products(side, first_chunk, past_chunk):
        a_ref = (a_mine, a_theirs)[side]

        def step(chunk, carry):
            results = []
            for u in range(UNROLL):
                code = q_list[chunk * UNROLL + u]
                ej = code // lay.n_slot
                ek = (ej // lay.p_slot) * lay.n_slot + code - ej * lay.n_slot
                high, low = split(a_ref[ek])
                right = jnp.concatenate([high, low, high], axis=0)
                results.append(
                    jnp.dot(left_ref[side * lay.blocks + ej], right, preferred_element_type=jnp.float32)
                )
            for u in range(UNROLL):
                q_ref[chunk * UNROLL + u] = results[u]
            return carry

        lax.fori_loop(first_chunk, past_chunk, step, 0)

    products(0, 0, count_ref[BUFFERS])
    products(1, count_ref[BUFFERS], count_ref[BUFFERS + 1])


def left_products(lay, counts, q_list, need, a_mine, a_theirs, p_mine, p_theirs):
    smem = pl.BlockSpec(memory_space=pltpu.SMEM)
    vmem = pl.BlockSpec(memory_space=pltpu.VMEM)
    return pl.pallas_call(
        functools.partial(left_kernel, lay),
        in_specs=[smem] * 3 + [vmem] * 4,
        out_specs=vmem,
        out_shape=jax.ShapeDtypeStruct((lay.most_q, lay.size, lay.size), jnp.float32),
        scratch_shapes=[pltpu.VMEM((2 * lay.blocks, lay.size, 3 * lay.size), jnp.bfloat16)],
        compiler_params=pltpu.CompilerParams(vmem_limit_bytes=VMEM_LIMIT),
        cost_estimate=work(5),
        name="left_products",
    )(counts, q_list, need, a_mine, a_theirs, p_mine, p_theirs)


def add_matches(lay, list_ref, count_ref, q_ref, p_refs, buffers, acc):
    for b, p_ref in zip(buffers, p_refs):

        def step(chunk, carry, b=b, p_ref=p_ref):
            results, outs = [], []
            for u in range(UNROLL):
                code = list_ref[b * lay.longest + chunk * UNROLL + u]
                outs.append(lax.bitwise_and(code, (1 << lay.o_bits) - 1))
                code = lax.shift_right_logical(code, lay.o_bits)
                at = lax.bitwise_and(code, (1 << lay.p_bits) - 1)
                q_high, q_low = split(q_ref[lax.shift_right_logical(code, lay.p_bits)])
                p_high, p_low = split(p_ref[at])
                left = jnp.concatenate([q_high, q_high, q_low], axis=1)
                right = jnp.concatenate([p_high, p_low, p_high], axis=0)
                results.append(jnp.dot(left, right, preferred_element_type=jnp.float32))
            for u in range(UNROLL):
                acc[outs[u]] += results[u]
            return carry

        lax.fori_loop(0, (count_ref[b] + UNROLL - 1) // UNROLL, step, 0)


def early_kernel(lay, list_ref, count_ref, q_ref, p0, p1, p2, p3, out_ref, acc):
    for i in range(lay.outs):
        acc[i] = jnp.zeros((lay.size, lay.size), jnp.float32)
    add_matches(lay, list_ref, count_ref, q_ref, (p0, p1, p2, p3), range(4), acc)
    for i in range(lay.outs):
        out_ref[i] = acc[i]


def late_kernel(lay, list_ref, count_ref, q_ref, p4, p5, part, *refs):
    outs, acc = refs[:6], refs[6]
    for i in range(lay.outs):
        acc[i] = part[i]
    add_matches(lay, list_ref, count_ref, q_ref, (p4, p5), range(4, 6), acc)
    for t in range(6):
        for i in range(lay.row_blocks):
            outs[t][i] = acc[t * lay.row_blocks + i]


def match_sums(kernel, lay, lists, counts, q_blocks, vectors, out_shape, cost, name):
    smem = pl.BlockSpec(memory_space=pltpu.SMEM)
    vmem = pl.BlockSpec(memory_space=pltpu.VMEM)
    return pl.pallas_call(
        functools.partial(kernel, lay),
        in_specs=[smem, smem] + [vmem] * (1 + len(vectors)),
        out_specs=[vmem] * len(out_shape),
        out_shape=out_shape,
        scratch_shapes=[pltpu.VMEM((lay.outs + 1, lay.size, lay.size), jnp.float32)],
        compiler_params=pltpu.CompilerParams(vmem_limit_bytes=VMEM_LIMIT),
        cost_estimate=work(cost),
        name=name,
    )(lists, counts, q_blocks, *vectors)


def per_device(
    a_blocks, neighbours, neighbour_count, p_blocks, p_columns, p_count, coarse_slot, coarse_pattern
):
    rows, groups = lax.axis_size("rows"), lax.axis_size("grp")
    e_local, n_slot, size = a_blocks.shape[:3]
    p_slot, pat = p_blocks.shape[1], coarse_pattern.shape[1]
    lay = Layout(e_local, n_slot, p_slot, size, pat, groups, coarse_slot.shape[0] // rows)
    row, grp = lax.axis_index("rows"), lax.axis_index("grp")
    upper, first, last = groups // 2, 0, groups - 1
    both = ("rows", "grp")
    core_pairs = [(g, g ^ 1) for g in range(groups)]
    upper_pairs = [(g, g ^ upper) for g in range(groups)]
    edges, inners = [first, last], [first ^ upper, last ^ upper]

    def along(g, step):
        return [
            (r * groups + g, (r + step) * groups + g)
            for r in range(rows)
            if 0 <= r + step < rows
        ]

    is_edge = (grp == first) | (grp == last)
    live = jnp.arange(p_slot, dtype=jnp.int32)[None, :] < p_count[:, None]
    own_live = jnp.where(live, p_columns, -1).reshape(-1)
    far_live = lax.ppermute(own_live, "grp", upper_pairs)
    rim_live = lax.ppermute(
        jnp.where(is_edge, own_live, far_live),
        both,
        along(last, 1) + along(first, -1) + along(last ^ upper, 1) + along(first ^ upper, -1),
    )
    mine = jnp.concatenate(
        [neighbours.reshape(-1), neighbour_count, p_columns.reshape(-1), p_count, own_live, far_live, rim_live]
    )
    theirs = lax.ppermute(mine, "grp", core_pairs)

    own = p_blocks.reshape(lay.blocks, size, size)
    a_mine = a_blocks.reshape(e_local * n_slot, size, size)
    crossed_first = lax.ppermute(own, "grp", [(g, g ^ upper) for g in edges])
    rim_direct = lax.ppermute(own, both, along(last, 1) + along(first, -1))
    own_core = lax.ppermute(own, "grp", core_pairs)
    a_theirs = lax.ppermute(a_mine, "grp", core_pairs)
    crossed_second = lax.ppermute(own, "grp", [(g, g ^ upper) for g in inners])
    rim_forward = lax.ppermute(crossed_first, both, along(last ^ upper, 1) + along(first ^ upper, -1))
    second = jnp.where(is_edge, rim_direct, crossed_first)
    second_core = lax.ppermute(second, "grp", core_pairs)
    third = jnp.where(is_edge, crossed_second, rim_forward)
    third_core = lax.ppermute(third, "grp", core_pairs)

    place = jnp.stack([row, grp]).astype(jnp.int32)
    lists, counts, q_list, need = match_lists(lay, place, mine, theirs, coarse_slot, coarse_pattern.reshape(-1))
    q_blocks = left_products(lay, counts, q_list, need, a_mine, a_theirs, own, own_core)
    blocks = lambda count: jax.ShapeDtypeStruct((count, size, size), jnp.float32)
    (part,) = match_sums(
        early_kernel, lay, lists, counts, q_blocks, [own, own_core, second, second_core], [blocks(lay.outs)], 5, "early"
    )
    kept_down, kept_here, kept_up, send_down, send_here, send_up = match_sums(
        late_kernel, lay, lists, counts, q_blocks, [third, third_core, part], [blocks(lay.row_blocks)] * 6, 3, "late"
    )
    down = kept_down + lax.ppermute(send_down, "grp", upper_pairs)
    up = kept_up + lax.ppermute(send_up, "grp", upper_pairs)
    here = kept_here + lax.ppermute(send_here, "grp", upper_pairs)
    from_next = lax.ppermute(down, "rows", [(r, r - 1) for r in range(1, rows)])
    from_prev = lax.ppermute(up, "rows", [(r, r + 1) for r in range(rows - 1)])
    return (here + from_next + from_prev).reshape(lay.per_owner, pat, size, size)


def solution(mesh):
    return jax.shard_map(
        per_device,
        mesh=mesh,
        in_specs=(
            P(("rows", "grp"), None, None, None),
            P(("rows", "grp"), None),
            P(("rows", "grp")),
            P(("rows", "grp"), None, None, None),
            P(("rows", "grp"), None),
            P(("rows", "grp")),
            P(),
            P(),
        ),
        out_specs=P(("rows", "grp"), None, None, None),
        check_vma=False,
    )
```
